128 devices in a mesh: row: 8 (over z, core), col: 16 (over y, x).
Axes of the slice: x: 4, y: 4, z: 4, core: 2. Of those that a mesh axis runs over, the one named last changes fastest.
Arguments:
- noise: bfloat16 [8192, 4096], P('row', 'col'), may hold values from -6 to 6
- data: bfloat16 [8192, 4096], P('col', 'row'), may hold values from -6 to 6
Outputs:
- targets: bfloat16 [8192, 4096], P('row', 'col')
- noise_potential: float32 [8192], P('row')
- data_potential: float32 [8192], P('col')
The draws below stay inside these ranges and needn't reach their ends.
All inputs are finite; a program needn't handle non-finite values.
Results may differ from the reference program's by a relative error of at most 0.0043.
Values may be sent and summed in bfloat16 or wider, within the bound.
No kernel may reach another device: no remote copies, remote signals or barrier semaphores. Data moves between devices by JAX's collectives and lax.ppermute only.
A program may use at most 128 MiB of HBM per device.

```python
import jax
import jax.numpy as jnp

D = 4096
ITERS = 4
NOISE = 8192
DATA = 8192


def draw_noise(key, part):
    own_key = jax.random.fold_in(key, 11)
    values = jnp.clip(jax.random.normal(own_key, (NOISE, D), jnp.float32), -6.0, 6.0)
    return values.astype(jnp.bfloat16)


def draw_data(key, part):
    own_key = jax.random.fold_in(key, 13)
    values = jnp.clip(jax.random.normal(own_key, (DATA, D), jnp.float32), -6.0, 6.0)
    return values.astype(jnp.bfloat16)


def setup_inputs(seed: int = 0) -> dict:
    streams_of = jax.random.split(jax.random.key(seed), 3)
    return {
        "noise": draw_noise(jax.random.fold_in(streams_of[2], 71), 0),
        "data": draw_data(jax.random.fold_in(streams_of[2], 71), 0),
    }


EPS = 0.02


def log_sum(z, axis):
    peak = jnp.max(z, axis=axis, keepdims=True)
    total = jnp.sum(jnp.exp(z - peak), axis=axis)
    return jnp.squeeze(peak, axis) + jnp.log(total)


def reference(noise, data):
    gram = jnp.dot(noise, data.T, preferred_element_type=jnp.float32)
    noise_sq = jnp.sum(noise.astype(jnp.float32) ** 2, axis=1)
    data_sq = jnp.sum(data.astype(jnp.float32) ** 2, axis=1)
    cost = (noise_sq[:, None] + data_sq[None, :] - 2.0 * gram) / D
    noise_potential = jnp.zeros((NOISE,), jnp.float32)
    data_potential = jnp.zeros((DATA,), jnp.float32)
    for step in range(ITERS):
        noise_potential = -EPS * jnp.log(float(NOISE)) - EPS * log_sum((data_potential[None, :] - cost) / EPS, 1)
        data_potential = -EPS * jnp.log(float(DATA)) - EPS * log_sum((noise_potential[:, None] - cost) / EPS, 0)
    scores = (data_potential[None, :] - cost) / EPS
    row_lse = log_sum(scores, 1)
    weights = jnp.exp(scores - row_lse[:, None]).astype(jnp.bfloat16)
    targets = jnp.dot(weights, data, preferred_element_type=jnp.float32).astype(jnp.bfloat16)
    return targets, noise_potential, data_potential
```

```python
import jax
import jax.numpy as jnp
from jax import lax
from jax.sharding import PartitionSpec as P

D = 4096
ITERS = 4


EPS = 0.02


def spread(values, axis):
    size = lax.axis_size(axis)
    copies = jnp.broadcast_to(values[None, None, :], (size, 1, values.shape[0]))
    return lax.all_to_all(copies, axis, 0, 0, tiled=True)[:, 0, :]


def lse(scores, axis):
    peak = jnp.max(scores, axis=axis, keepdims=True)
    total = jnp.sum(jnp.exp(scores - peak), axis=axis)
    return jnp.squeeze(peak, axis) + jnp.log(total)


def row_logsum(scores):
    return lse(spread(lse(scores, 1), "col"), 0)


def col_logsum(scores):
    return lse(spread(lse(scores, 0), "row"), 0)


def local(noise, data):
    data_whole = lax.all_gather(data, "row", axis=1, tiled=True)
    data_sq = jnp.sum(data_whole.astype(jnp.float32) ** 2, axis=1)
    rows_here = noise.shape[0]
    noise_whole = lax.all_gather(noise, "col", axis=1, tiled=True)
    gram = lax.dot_general(
        noise_whole, data_whole, (((1,), (1,)), ((), ())), preferred_element_type=jnp.float32
    )
    noise_sq = jnp.sum(noise_whole.astype(jnp.float32) ** 2, axis=1)
    cost = (noise_sq[:, None] + data_sq[None, :] - 2.0 * gram) / D
    noise_count = float(rows_here * lax.axis_size("row"))
    data_count = float(data_whole.shape[0] * lax.axis_size("col"))
    noise_potential = jnp.zeros((rows_here,), jnp.float32)
    data_potential = jnp.zeros((data_whole.shape[0],), jnp.float32)
    for step in range(ITERS):
        noise_potential = -EPS * jnp.log(noise_count) - EPS * row_logsum(
            (data_potential[None, :] - cost) / EPS
        )
        data_potential = -EPS * jnp.log(data_count) - EPS * col_logsum(
            (noise_potential[:, None] - cost) / EPS
        )
    scores = (data_potential[None, :] - cost) / EPS
    row_lse = row_logsum(scores)
    weights = jnp.exp(scores - row_lse[:, None]).astype(jnp.bfloat16)
    partial_targets = jnp.dot(weights, data_whole, preferred_element_type=jnp.float32)
    targets = lax.psum_scatter(partial_targets, "col", scatter_dimension=1, tiled=True).astype(
        jnp.bfloat16
    )
    return (targets, noise_potential, data_potential)


def solution(mesh):
    placed = (P("row", "col"), P("col", "row"))
    return jax.shard_map(
        local,
        mesh=mesh,
        in_specs=placed,
        out_specs=(P("row", "col"), P("row"), P("col")),
        check_vma=False,
    )
```

```python
import functools

import jax
import jax.numpy as jnp
from jax import lax
from jax.experimental import pallas as pl
from jax.experimental.pallas import tpu as pltpu
from jax.sharding import PartitionSpec as P

D = 4096
ITERS = 4
COUNT = 8192
EPS = 0.02

AXES = ("row", "col")
PLACES = [(z, c, y, x) for z in range(4) for c in range(2) for y in range(4) for x in range(4)]


def flat(z, c, y, x):
    return ((z % 4 * 2 + c % 2) * 4 + y % 4) * 4 + x % 4


def pairs(move):
    return [(flat(*p), flat(*move(*p))) for p in PLACES]


def groups(shared):
    found = {}
    for p in PLACES:
        key = tuple(v for v, name in zip(p, "zcyx") if name in shared)
        found.setdefault(key, []).append(flat(*p))
    return list(found.values())


OTHER = pairs(lambda z, c, y, x: (z, c + 1, y, x))
X_UP = pairs(lambda z, c, y, x: (z, c, y, x + 1))
X_DOWN = pairs(lambda z, c, y, x: (z, c, y, x - 1))
FIRST_UP = pairs(lambda z, c, y, x: (z + 1 - c, c, y + c, x))
FIRST_DOWN = pairs(lambda z, c, y, x: (z - 1 + c, c, y - c, x))
SECOND_UP = pairs(lambda z, c, y, x: (z + c, c, y + 1 - c, x))
SECOND_DOWN = pairs(lambda z, c, y, x: (z - c, c, y - 1 + c, x))


def send(values, where):
    return lax.ppermute(values, AXES, where)


def spread(values, size, shared):
    copies = jnp.broadcast_to(values[None, None, :], (size, 1, values.shape[0]))
    return lax.all_to_all(
        copies, AXES, 0, 0, tiled=True, axis_index_groups=groups(shared)
    )[:, 0, :]


def ring(block, up, down):
    half = block.shape[0] // 2
    below, above = send(block, up), send(block, down)
    far = jnp.concatenate([send(below[:half], up), send(above[half:], down)])
    return [block, above, far, below]


def lse(scores, axis):
    peak = jnp.max(scores, axis=axis, keepdims=True)
    total = jnp.sum(jnp.exp(scores - peak), axis=axis)
    return jnp.squeeze(peak, axis) + jnp.log(total)


def block_place(place, first, second):
    z, c, y = place[0], place[1], place[2]
    far_z = jnp.where(c == 0, first, second)
    far_y = jnp.where(c == 0, second, first)
    return lax.rem(y + far_y, 4), lax.rem(z + far_z, 4)


def gram_kernel(seconds, first_call, place, own, other, *refs):
    blocks = refs[: len(seconds)]
    gram_in, squares_in = (None, None) if first_call else refs[len(seconds) : len(seconds) + 2]
    gram, squares = refs[-2:]
    step = pl.program_id(0)

    @pl.when(step == 0)
    def _():
        gram[...] = jnp.zeros_like(gram) if first_call else gram_in[...]
        squares[...] = jnp.zeros_like(squares) if first_call else squares_in[...]

    c, x = place[1], place[3]
    for second, block in zip(seconds, blocks):
        row_group, col_group = block_place(place, step, second)
        rows = pl.ds(pl.multiple_of(row_group * 256, 256), 256)
        sums = [None, None]
        total = None
        for part in range(4):
            values = block[0, :, part * 256 : (part + 1) * 256]
            index = lax.rem(part + 4 - x, 4) * 4 + col_group
            for k, source in enumerate((own, other)):
                term = lax.dot_general(
                    source[index], values, (((1,), (1,)), ((), ())), preferred_element_type=jnp.float32
                )
                sums[k] = term if part == 0 else sums[k] + term
            wide = values.astype(jnp.float32)
            wide = wide * wide
            halves = wide[:, :128] + wide[:, 128:]
            total = halves if part == 0 else total + halves
        squares[rows, :] += total
        gram[pl.ds(pl.multiple_of(c * 256, 256), 256), rows] += sums[0]
        gram[pl.ds(pl.multiple_of(256 - c * 256, 256), 256), rows] += sums[1]


def gram_of(place, own, other, blocks, seconds, before):
    whole = lambda shape: pl.BlockSpec(shape, lambda i, place: (0,) * len(shape))
    specs = [whole((16, 256, 256))] * 2
    specs += [pl.BlockSpec((1, 256, 1024), lambda i, place: (i, 0, 0))] * len(blocks)
    outs = [((512, 1024), jnp.float32), ((1024, 128), jnp.float32)]
    operands = [own, other, *blocks]
    aliases = {}
    if before is not None:
        aliases = {1 + len(operands): 0, 2 + len(operands): 1}
        operands += before
        specs += [whole(shape) for shape, _ in outs]
    return pl.pallas_call(
        functools.partial(gram_kernel, seconds, before is None),
        out_shape=[jax.ShapeDtypeStruct(*out) for out in outs],
        grid_spec=pltpu.PrefetchScalarGridSpec(
            num_scalar_prefetch=1,
            grid=(4,),
            in_specs=specs,
            out_specs=[whole(shape) for shape, _ in outs],
        ),
        input_output_aliases=aliases,
        compiler_params=pltpu.CompilerParams(vmem_limit_bytes=40 * 2**20),
        cost_estimate=pl.CostEstimate(
            flops=len(blocks) * 4 * 2 * 512 * 256 * 1024,
            bytes_accessed=len(blocks) * 2 * 2**20 + 8 * 2**20,
            transcendentals=0,
        ),
    )(place, *operands)


def mix_kernel(place, weights, *refs):
    blocks, out, sums = refs[:4], refs[4], refs[5]
    step = pl.program_id(0)

    @pl.when(step == 0)
    def _():
        sums[...] = jnp.zeros_like(sums)

    for second, block in enumerate(blocks):
        row_group, col_group = block_place(place, step, second)
        left = weights[:, pl.ds(pl.multiple_of(row_group * 256, 256), 256)]
        for part in range(4):
            sums[col_group * 4 + part] += jnp.dot(
                left, block[0, :, part * 256 : (part + 1) * 256], preferred_element_type=jnp.float32
            )

    @pl.when(step == 3)
    def _():
        out[...] = sums[...].astype(out.dtype)


def mix(place, weights, blocks, dtype):
    whole = lambda shape: pl.BlockSpec(shape, lambda i, place: (0,) * len(shape))
    return pl.pallas_call(
        mix_kernel,
        out_shape=jax.ShapeDtypeStruct((16, 256, 256), dtype),
        grid_spec=pltpu.PrefetchScalarGridSpec(
            num_scalar_prefetch=1,
            grid=(4,),
            in_specs=[whole((256, 1024))]
            + [pl.BlockSpec((1, 256, 1024), lambda i, place: (i, 0, 0))] * 4,
            out_specs=whole((16, 256, 256)),
            scratch_shapes=[pltpu.VMEM((16, 256, 256), jnp.float32)],
        ),
        compiler_params=pltpu.CompilerParams(vmem_limit_bytes=40 * 2**20),
        cost_estimate=pl.CostEstimate(
            flops=2 * 256 * 1024 * 4096, bytes_accessed=14 * 2**20, transcendentals=0
        ),
    )(place, weights, *blocks)


def local(noise, data):
    row, col = lax.axis_index("row"), lax.axis_index("col")
    z, c, y, x = row // 2, row % 2, col // 4, col % 4
    place = jnp.stack([z, c, y, x]).astype(jnp.int32)

    halves = data.reshape(2, 256, 512)
    kept = lax.dynamic_index_in_dim(halves, c, 0, keepdims=False)
    came = send(lax.dynamic_index_in_dim(halves, 1 - c, 0, keepdims=False), OTHER)
    block = jnp.where(
        c == 0, jnp.concatenate([kept, came], 1), jnp.concatenate([came, kept], 1)
    )
    line = jnp.stack(ring(block, FIRST_UP, FIRST_DOWN))
    own = lax.all_to_all(
        noise.reshape(4, 256, 256), AXES, 0, 0, tiled=True, axis_index_groups=groups("zcx")
    )
    own = jnp.concatenate(ring(own, X_UP, X_DOWN))
    other = send(own, OTHER)
    blocks = ring(line, SECOND_UP, SECOND_DOWN)

    parts = gram_of(place, own, other, blocks[:1], (0,), None)
    parts = gram_of(place, own, other, [blocks[1], blocks[3]], (1, 3), parts)
    gram, squares = gram_of(place, own, other, blocks[2:3], (2,), parts)

    def square_sum(values):
        return jnp.sum(values.astype(jnp.float32) ** 2, axis=(0, 2))

    sq_own, sq_other = square_sum(own), square_sum(other)
    noise_sq = jnp.where(
        c == 0, jnp.concatenate([sq_own, sq_other]), jnp.concatenate([sq_other, sq_own])
    )
    data_sq = jnp.sum(squares, axis=1)
    scores = (2.0 * gram - noise_sq[:, None] - data_sq[None, :]) / (D * EPS)

    def row_lse(g):
        return lse(spread(lse(scores + g[None, :], 1), 8, "zy"), 0)

    log_count = jnp.log(float(COUNT))
    g = jnp.zeros((1024,), jnp.float32)
    for step in range(ITERS):
        f = -log_count - row_lse(g)
        g = -log_count - lse(spread(lse(scores + f[:, None], 0), 16, "cx"), 0)
    norm = row_lse(g)
    weights = jnp.exp(scores + g[None, :] - norm[:, None]).astype(jnp.bfloat16)
    weights = weights.reshape(2, 256, 1024)

    away = mix(place, lax.dynamic_index_in_dim(weights, 1 - c, 0, keepdims=False), blocks, jnp.bfloat16)
    came = send(away, OTHER)
    mine = mix(place, lax.dynamic_index_in_dim(weights, c, 0, keepdims=False), blocks, jnp.float32)
    shares = (mine + came.astype(jnp.float32)).astype(jnp.bfloat16)
    shares = lax.all_to_all(shares, "col", 0, 0, tiled=True)
    targets = jnp.sum(shares.reshape(4, 4, 256, 256).astype(jnp.float32), axis=1)
    targets = targets.reshape(1024, 256).astype(jnp.bfloat16)

    f_here = lax.dynamic_slice(f, (c * 256,), (256,))
    noise_potential = EPS * spread(f_here, 4, "zcx").reshape(1024)
    g_here = lax.dynamic_slice(g, (y * 256,), (256,))
    g_came = send(g_here, OTHER)
    data_potential = EPS * jnp.where(
        c == 0, jnp.concatenate([g_here, g_came]), jnp.concatenate([g_came, g_here])
    )
    return (targets, noise_potential, data_potential)


def solution(mesh):
    placed = (P("row", "col"), P("col", "row"))
    return jax.shard_map(
        local,
        mesh=mesh,
        in_specs=placed,
        out_specs=(P("row", "col"), P("row"), P("col")),
        check_vma=False,
    )
```

```python
import functools

import jax
import jax.numpy as jnp
from jax import lax
from jax.experimental import pallas as pl
from jax.experimental.pallas import tpu as pltpu
from jax.sharding import PartitionSpec as P

D = 4096
ITERS = 4
COUNT = 8192
EPS = 0.02

AXES = ("row", "col")
PLACES = [(z, c, y, x) for z in range(4) for c in range(2) for y in range(4) for x in range(4)]


def flat(z, c, y, x):
    return ((z % 4 * 2 + c % 2) * 4 + y % 4) * 4 + x % 4


def pairs(move):
    return [(flat(*p), flat(*move(*p))) for p in PLACES]


def groups(shared):
    found = {}
    for p in PLACES:
        key = tuple(v for v, name in zip(p, "zcyx") if name in shared)
        found.setdefault(key, []).append(flat(*p))
    return list(found.values())


OTHER = pairs(lambda z, c, y, x: (z, c + 1, y, x))
Y_DOWN = [pairs(lambda z, c, y, x, k=k: (z, c, y - k, x)) for k in range(4)]
X_UP = pairs(lambda z, c, y, x: (z, c, y, x + 1))
X_DOWN = pairs(lambda z, c, y, x: (z, c, y, x - 1))
FIRST_UP = pairs(lambda z, c, y, x: (z + 1 - c, c, y + c, x))
FIRST_DOWN = pairs(lambda z, c, y, x: (z - 1 + c, c, y - c, x))
SECOND_UP = pairs(lambda z, c, y, x: (z + c, c, y + 1 - c, x))
SECOND_DOWN = pairs(lambda z, c, y, x: (z - c, c, y - 1 + c, x))


def send(values, where):
    return lax.ppermute(values, AXES, where)


def spread(values, size, shared):
    copies = jnp.broadcast_to(values[None, None, :], (size, 1, values.shape[0]))
    return lax.all_to_all(
        copies, AXES, 0, 0, tiled=True, axis_index_groups=groups(shared)
    )[:, 0, :]


def ring(block, up, down):
    half = block.shape[0] // 2
    below, above = send(block, up), send(block, down)
    far = jnp.concatenate([send(below[:half], up), send(above[half:], down)])
    return [block, above, far, below]


def lse(scores, axis):
    peak = jnp.max(scores, axis=axis, keepdims=True)
    total = jnp.sum(jnp.exp(scores - peak), axis=axis)
    return jnp.squeeze(peak, axis) + jnp.log(total)


def place_of(place, piece):
    z, c, y = place[0], place[1], place[2]
    first, second = piece
    far_z = jnp.where(c == 0, first, second)
    far_y = jnp.where(c == 0, second, first)
    return lax.rem(y + far_y, 4), lax.rem(z + far_z, 4)


def load(refs, spans, part):
    columns = slice(part * 256, (part + 1) * 256)
    values = [refs[k][start : start + rows, columns] for k, start, rows in spans]
    return values[0] if len(values) == 1 else jnp.concatenate(values)


def gram_kernel(pieces, count, first_call, place, own, other, *refs):
    blocks = refs[:count]
    gram, squares = refs[-2:]
    if first_call:
        gram[...] = jnp.zeros_like(gram)
        squares[...] = jnp.zeros_like(squares)
    else:
        gram[...] = refs[count][...]
        squares[...] = refs[count + 1][...]
    c, y, x = place[1], place[2], place[3]
    for where, spans in pieces:
        row_group, col_group = place_of(place, where)
        rows = pl.ds(pl.multiple_of(row_group * 256, 256), 256)
        sums = [None, None]
        total = None
        for part in range(4):
            values = load(blocks, spans, part)
            index = lax.rem(part + 4 - x, 4) * 4 + lax.rem(col_group + 4 - y, 4)
            for k, source in enumerate((own, other)):
                term = lax.dot_general(
                    source[index], values, (((1,), (1,)), ((), ())), preferred_element_type=jnp.float32
                )
                sums[k] = term if part == 0 else sums[k] + term
            wide = values.astype(jnp.float32)
            wide = wide * wide
            halves = wide[:, :128] + wide[:, 128:]
            total = halves if part == 0 else total + halves
        squares[rows, :] += total
        gram[pl.ds(pl.multiple_of(c * 256, 256), 256), rows] += sums[0]
        gram[pl.ds(pl.multiple_of(256 - c * 256, 256), 256), rows] += sums[1]


def gram_of(place, own, other, arrays, pieces, before):
    outs = [((512, 1024), jnp.float32), ((1024, 128), jnp.float32)]
    operands = [own, other, *arrays, *(before or [])]
    return pl.pallas_call(
        functools.partial(gram_kernel, pieces, len(arrays), before is None),
        out_shape=[jax.ShapeDtypeStruct(*out) for out in outs],
        in_specs=[pl.BlockSpec(memory_space=pltpu.SMEM)]
        + [pl.BlockSpec(memory_space=pltpu.VMEM)] * len(operands),
        out_specs=[pl.BlockSpec(memory_space=pltpu.VMEM)] * 2,
        compiler_params=pltpu.CompilerParams(vmem_limit_bytes=24 * 2**20),
        cost_estimate=pl.CostEstimate(
            flops=len(pieces) * 2 * 512 * 256 * 1024,
            bytes_accessed=len(pieces) * 2**19 + 8 * 2**20,
            transcendentals=0,
        ),
    )(place, *operands)


def mix_kernel(pieces, away, place, weights, *refs):
    blocks, out, sums = refs[: len(refs) - 2 - (not away)], refs[-2], refs[-1]
    half = place[1] if not away else 1 - place[1]
    rows = pl.ds(pl.multiple_of(half * 256, 256), 256)
    sums[...] = jnp.zeros_like(sums)
    for where, spans in pieces:
        row_group, col_group = place_of(place, where)
        left = weights[rows, pl.ds(pl.multiple_of(row_group * 256, 256), 256)]
        for part in range(4):
            sums[col_group * 4 + part] += jnp.dot(
                left, load(blocks, spans, part), preferred_element_type=jnp.float32
            )
    total = sums[...]
    if not away:
        total = total + refs[-3][...].astype(jnp.float32)
    out[...] = total.astype(out.dtype)


def mix(place, weights, arrays, pieces, came):
    operands = [weights, *arrays, *([] if came is None else [came])]
    return pl.pallas_call(
        functools.partial(mix_kernel, pieces, came is None),
        out_shape=jax.ShapeDtypeStruct((16, 256, 256), jnp.bfloat16),
        in_specs=[pl.BlockSpec(memory_space=pltpu.SMEM)]
        + [pl.BlockSpec(memory_space=pltpu.VMEM)] * len(operands),
        out_specs=pl.BlockSpec(memory_space=pltpu.VMEM),
        scratch_shapes=[pltpu.VMEM((16, 256, 256), jnp.float32)],
        compiler_params=pltpu.CompilerParams(vmem_limit_bytes=32 * 2**20),
        cost_estimate=pl.CostEstimate(
            flops=2 * 256 * 1024 * 4096, bytes_accessed=14 * 2**20, transcendentals=0
        ),
    )(place, *operands)


def local(noise, data):
    row, col = lax.axis_index("row"), lax.axis_index("col")
    z, c, y, x = row // 2, row % 2, col // 4, col % 4
    place = jnp.stack([z, c, y, x]).astype(jnp.int32)

    halves = data.reshape(2, 256, 512)
    kept = lax.dynamic_index_in_dim(halves, c, 0, keepdims=False)
    came = send(lax.dynamic_index_in_dim(halves, 1 - c, 0, keepdims=False), OTHER)
    block = jnp.where(
        c == 0, jnp.concatenate([kept, came], 1), jnp.concatenate([came, kept], 1)
    )
    below, above = send(block, FIRST_UP), send(block, FIRST_DOWN)
    own_below, own_above = send(block, SECOND_UP), send(block, SECOND_DOWN)
    far = jnp.concatenate([send(below[:128], FIRST_UP), send(above[128:], FIRST_DOWN)])
    near = jnp.concatenate([below, above])
    near_below, near_above = send(near, SECOND_UP), send(near, SECOND_DOWN)
    far_below = send(jnp.concatenate([far, own_below[:128]]), SECOND_UP)
    far_above = send(jnp.concatenate([far, own_above[128:]]), SECOND_DOWN)
    near_far = [send(near_below[:256], SECOND_UP), send(near_above[256:], SECOND_DOWN)]
    far_far = [send(far_below[:128], SECOND_UP), send(far_above[128:256], SECOND_DOWN)]
    parts = noise.reshape(4, 256, 256)
    own = [
        send(lax.dynamic_index_in_dim(parts, (y + 4 - k) % 4, 0, keepdims=False), Y_DOWN[k])
        if k
        else lax.dynamic_index_in_dim(parts, y, 0, keepdims=False)
        for k in range(4)
    ]
    own = jnp.concatenate(ring(jnp.stack(own), X_UP, X_DOWN))
    other = send(own, OTHER)

    whole = lambda k, start=0: [(k, start, 256)]
    arrays = [block, below, above, own_below, own_above, far]
    places = [(0, 0), (3, 0), (1, 0), (0, 3), (0, 1), (2, 0)]
    stages = [(arrays, [(p, whole(k)) for k, p in enumerate(places)])]
    stages.append(
        (
            [near_below, near_above],
            [((3, 3), whole(0)), ((1, 3), whole(0, 256)), ((3, 1), whole(1)), ((1, 1), whole(1, 256))],
        )
    )
    stages.append(
        (
            [far_below, far_above],
            [((2, 3), whole(0)), ((2, 1), whole(1)), ((0, 2), [(0, 256, 128), (1, 256, 128)])],
        )
    )
    stages.append(
        (
            near_far + far_far,
            [((3, 2), whole(0)), ((1, 2), whole(1)), ((2, 2), [(2, 0, 128), (3, 0, 128)])],
        )
    )
    sums, all_arrays, all_pieces = None, [], []
    for arrays, pieces in stages:
        sums = gram_of(place, own, other, arrays, pieces, sums)
        offset = len(all_arrays)
        all_pieces += [(p, [(k + offset, start, rows) for k, start, rows in spans]) for p, spans in pieces]
        all_arrays += arrays
    gram, squares = sums

    def square_sum(values):
        return jnp.sum(values.astype(jnp.float32) ** 2, axis=(0, 2))

    sq_own, sq_other = square_sum(own), square_sum(other)
    noise_sq = jnp.where(
        c == 0, jnp.concatenate([sq_own, sq_other]), jnp.concatenate([sq_other, sq_own])
    )
    data_sq = jnp.sum(squares, axis=1)
    scores = (2.0 * gram - noise_sq[:, None] - data_sq[None, :]) / (D * EPS)

    def row_lse(g):
        return lse(spread(lse(scores + g[None, :], 1), 8, "zy"), 0)

    log_count = jnp.log(float(COUNT))
    g = jnp.zeros((1024,), jnp.float32)
    for step in range(ITERS):
        f = -log_count - row_lse(g)
        g = -log_count - lse(spread(lse(scores + f[:, None], 0), 16, "cx"), 0)
    norm = row_lse(g)
    weights = jnp.exp(scores + g[None, :] - norm[:, None]).astype(jnp.bfloat16)
    away = mix(place, weights, all_arrays, all_pieces, None)
    shares = mix(place, weights, all_arrays, all_pieces, send(away, OTHER))
    f, g, shares = lax.optimization_barrier((f, g, shares))
    shares = lax.all_to_all(shares, "col", 0, 0, tiled=True)
    targets = jnp.sum(shares.reshape(4, 4, 256, 256).astype(jnp.float32), axis=1)
    targets = targets.reshape(1024, 256).astype(jnp.bfloat16)

    f_here = lax.dynamic_slice(f, (c * 256,), (256,))
    noise_potential = EPS * spread(f_here, 4, "zcx").reshape(1024)
    g_here = lax.dynamic_slice(g, (y * 256,), (256,))
    g_came = send(g_here, OTHER)
    data_potential = EPS * jnp.where(
        c == 0, jnp.concatenate([g_here, g_came]), jnp.concatenate([g_came, g_here])
    )
    return (targets, noise_potential, data_potential)


def solution(mesh):
    placed = (P("row", "col"), P("col", "row"))
    return jax.shard_map(
        local,
        mesh=mesh,
        in_specs=placed,
        out_specs=(P("row", "col"), P("row"), P("col")),
        check_vma=False,
    )
```

```python
import functools

import jax
import jax.numpy as jnp
from jax import lax
from jax.experimental import pallas as pl
from jax.experimental.pallas import tpu as pltpu
from jax.sharding import PartitionSpec as P

D = 4096
ITERS = 4
COUNT = 8192
EPS = 0.02

AXES = ("row", "col")
PLACES = [(z, c, y, x) for z in range(4) for c in range(2) for y in range(4) for x in range(4)]


def flat(z, c, y, x):
    return ((z % 4 * 2 + c % 2) * 4 + y % 4) * 4 + x % 4


def pairs(move):
    return [(flat(*p), flat(*move(*p))) for p in PLACES]


def groups(shared):
    found = {}
    for p in PLACES:
        key = tuple(v for v, name in zip(p, "zcyx") if name in shared)
        found.setdefault(key, []).append(flat(*p))
    return list(found.values())


OTHER = pairs(lambda z, c, y, x: (z, c + 1, y, x))
FIRST_UP = pairs(lambda z, c, y, x: (z + 1 - c, c, y + c, x))
FIRST_DOWN = pairs(lambda z, c, y, x: (z - 1 + c, c, y - c, x))
FIRST_TWO = pairs(lambda z, c, y, x: (z + 2 - 2 * c, c, y + 2 * c, x))
SECOND_UP = pairs(lambda z, c, y, x: (z + c, c, y + 1 - c, x))
SECOND_DOWN = pairs(lambda z, c, y, x: (z - c, c, y - 1 + c, x))


def send(values, where):
    return lax.ppermute(values, AXES, where)


def spread(values, size, shared):
    copies = jnp.broadcast_to(values[None, None, :], (size, 1, values.shape[0]))
    return lax.all_to_all(
        copies, AXES, 0, 0, tiled=True, axis_index_groups=groups(shared)
    )[:, 0, :]


def lse(scores, axis):
    peak = jnp.max(scores, axis=axis, keepdims=True)
    total = jnp.sum(jnp.exp(scores - peak), axis=axis)
    return jnp.squeeze(peak, axis) + jnp.log(total)


def place_of(place, piece):
    z, c, y = place[0], place[1], place[2]
    first, second = piece
    far_z = jnp.where(c == 0, first, second)
    far_y = jnp.where(c == 0, second, first)
    return lax.rem(y + far_y, 4), lax.rem(z + far_z, 4)


HIGHEST = lax.Precision.HIGHEST
BLOCKS = 8


def gram_kernel(pieces, sides, first_call, last_call, place, *refs):
    count = len(pieces)
    sources, held = refs[: len(sides)], refs[len(sides) : len(sides) + count]
    outs, state_in = refs[-3:], refs[-6:-3]
    c = place[1]
    halves = [pl.ds(pl.multiple_of(k, 256), 256) for k in (c * 256, 256 - c * 256)]
    gram, squares, noise_squares = outs
    if first_call:
        gram[...] = jnp.zeros_like(gram)
        squares[...] = jnp.zeros_like(squares)
        noise_squares[...] = jnp.zeros_like(noise_squares)
    else:
        for k in range(3):
            outs[k][...] = state_in[k][...]
    if not last_call:
        total = jnp.zeros((256, 128), jnp.float32)
        for k in range(16):
            wide = sources[0][k].astype(jnp.float32)
            wide = wide * wide
            total = total + wide[:, :128] + wide[:, 128:]
        noise_squares[halves[sides[0]], :] = total
    for k, pair in enumerate(pieces):
        for side, where in enumerate(pair):
            row_group, col_group = place_of(place, where)
            rows = pl.ds(pl.multiple_of(row_group * 256, 256), 256)
            sums = [None] * len(sides)
            total = None
            for part in range(4):
                values = held[k][side * 256 : side * 256 + 256, part * 256 : part * 256 + 256]
                for n in range(len(sides)):
                    term = lax.dot_general(
                        sources[n][part * 4 + col_group],
                        values,
                        (((1,), (1,)), ((), ())),
                        preferred_element_type=jnp.float32,
                    )
                    sums[n] = term if part == 0 else sums[n] + term
                if sides[0] == 0:
                    wide = values.astype(jnp.float32)
                    wide = wide * wide
                    folded = wide[:, :128] + wide[:, 128:]
                    total = folded if part == 0 else total + folded
            if sides[0] == 0:
                squares[rows, :] += total
            for n, half in enumerate(sides):
                gram[halves[half], rows] += sums[n]
    if last_call:
        data_sq = lax.dot_general(
            jnp.ones((8, 128), jnp.float32),
            squares[...],
            (((1,), (1,)), ((), ())),
            precision=HIGHEST,
            preferred_element_type=jnp.float32,
        )[0:1, :]
        noise_sq = jnp.sum(noise_squares[...], axis=1, keepdims=True)
        gram[...] = (2.0 * gram[...] - noise_sq - data_sq) * (1.0 / (D * EPS))


def gram_of(place, sources, sides, arrays, pieces, before, last_call):
    outs = [(512, 1024), (1024, 128), (512, 128)]
    count = len(arrays)
    operands = [*sources, *arrays, *(before or [])]
    vmem = pl.BlockSpec(memory_space=pltpu.VMEM)
    aliases = {} if before is None else {len(operands) - 2 + k: k for k in range(3)}
    return pl.pallas_call(
        functools.partial(gram_kernel, pieces, sides, before is None, last_call),
        out_shape=[jax.ShapeDtypeStruct(shape, jnp.float32) for shape in outs],
        in_specs=[pl.BlockSpec(memory_space=pltpu.SMEM)] + [vmem] * len(operands),
        out_specs=[vmem] * 3,
        input_output_aliases=aliases,
        compiler_params=pltpu.CompilerParams(vmem_limit_bytes=28 * 2**20),
        cost_estimate=pl.CostEstimate(
            flops=count * len(sides) * 2 * 512 * 256 * 1024,
            bytes_accessed=count * 2**20 + 8 * 2**20,
            transcendentals=0,
        ),
    )(place, *operands)


def mix_kernel(pieces, away, place, weights, *refs):
    held, out, buffer, sems = refs[:BLOCKS], refs[-3], refs[-2], refs[-1]
    copies = []
    for k, pair in enumerate(pieces):
        for side, where in enumerate(pair):
            row_group, col_group = place_of(place, where)
            rows = pl.ds(pl.multiple_of(row_group * 256, 256), 256)
            columns = pl.ds(pl.multiple_of(col_group * 1024, 1024), 1024)
            copies.append(
                pltpu.make_async_copy(
                    held[k].at[pl.ds(side * 256, 256)], buffer.at[rows, columns], sems.at[2 * k + side]
                )
            )
    for copy in copies:
        copy.start()
    half = place[1] if not away else 1 - place[1]
    left = weights[pl.ds(pl.multiple_of(half * 256, 256), 256), :]
    for copy in copies:
        copy.wait()
    for n in range(16):
        total = jnp.dot(left, buffer[:, n * 256 : n * 256 + 256], preferred_element_type=jnp.float32)
        if not away:
            total = total + refs[BLOCKS][n].astype(jnp.float32)
        out[n] = total.astype(out.dtype)


def mix(place, weights, arrays, pieces, came):
    vmem = pl.BlockSpec(memory_space=pltpu.VMEM)
    operands = [weights, *arrays, *([] if came is None else [came])]
    return pl.pallas_call(
        functools.partial(mix_kernel, pieces, came is None),
        out_shape=jax.ShapeDtypeStruct((16, 256, 256), jnp.bfloat16),
        in_specs=[pl.BlockSpec(memory_space=pltpu.SMEM), vmem]
        + [pl.BlockSpec(memory_space=pl.ANY)] * BLOCKS
        + [vmem] * (came is not None),
        out_specs=vmem,
        scratch_shapes=[
            pltpu.VMEM((1024, 4096), jnp.bfloat16),
            pltpu.SemaphoreType.DMA((2 * BLOCKS,)),
        ],
        compiler_params=pltpu.CompilerParams(vmem_limit_bytes=32 * 2**20),
        cost_estimate=pl.CostEstimate(
            flops=2 * 256 * 1024 * 4096, bytes_accessed=14 * 2**20, transcendentals=0
        ),
    )(place, *operands)


def local(noise, data):
    row, col = lax.axis_index("row"), lax.axis_index("col")
    z, c, y, x = row // 2, row % 2, col // 4, col % 4
    place = jnp.stack([z, c, y, x]).astype(jnp.int32)

    halves = data.reshape(2, 256, 512)
    kept = lax.dynamic_index_in_dim(halves, c, 0, keepdims=False)
    came = send(lax.dynamic_index_in_dim(halves, 1 - c, 0, keepdims=False), OTHER)
    block = jnp.where(
        c == 0, jnp.concatenate([kept, came], 1), jnp.concatenate([came, kept], 1)
    )
    below, above, far = lax.optimization_barrier(
        (send(block, FIRST_UP), send(block, FIRST_DOWN), send(block, FIRST_TWO))
    )
    own = lax.all_to_all(
        noise.reshape(4, 256, 256), AXES, 0, 0, tiled=True, axis_index_groups=groups("zcx")
    )
    own = lax.all_to_all(
        jnp.broadcast_to(own[None], (4, 4, 256, 256)).reshape(4, 1024, 256),
        AXES,
        0,
        0,
        tiled=True,
        axis_index_groups=groups("zcy"),
    ).reshape(16, 256, 256)
    one, two = jnp.concatenate([block, below]), jnp.concatenate([above, far])
    one_below, two_above = send(one, SECOND_UP), send(two, SECOND_DOWN)
    one_above, two_below = send(one, SECOND_DOWN), send(two, SECOND_UP)
    one_below, two_above, one_above, two_below, own = lax.optimization_barrier(
        (one_below, two_above, one_above, two_below, own)
    )
    other = send(own, OTHER)
    one_far, two_far = send(one_below, SECOND_UP), send(two_above, SECOND_DOWN)

    arrays = [one, two, one_above, two_below, one_below, two_above, one_far, two_far]
    pieces = [
        [(first, second) for first in ((0, 3), (1, 2))[k % 2]] for k, second in enumerate((0, 0, 1, 3, 3, 1, 2, 2))
    ]
    state = gram_of(place, [own], (0,), arrays[:6], pieces[:6], None, False)
    state = gram_of(place, [other], (1,), arrays[:6], pieces[:6], state, False)
    scores = gram_of(place, [own, other], (0, 1), arrays[6:], pieces[6:], state, True)[0]

    def row_exchange(g, extra):
        mine = lse(scores + g[None, :], 1)
        shared = spread(jnp.concatenate([mine, extra]), 8, "zy")
        return lse(shared[:, :512], 0), shared[:, 512:]

    def col_exchange(f, extra):
        mine = lse(scores + f[:, None], 0)
        shared = spread(jnp.concatenate([mine, extra]), 16, "cx")
        return lse(shared[:, :1024], 0), shared[:, 1024:]

    log_count = jnp.log(float(COUNT))
    nothing = jnp.zeros((0,), jnp.float32)
    g = jnp.zeros((1024,), jnp.float32)
    for step in range(ITERS):
        f = -log_count - row_exchange(g, nothing)[0]
        total, all_f = col_exchange(f, nothing if step < ITERS - 1 else f)
        g = -log_count - total
    norm, all_g = row_exchange(g, lax.dynamic_slice(g, (y * 256,), (256,)))
    weights = jnp.exp(scores + g[None, :] - norm[:, None]).astype(jnp.bfloat16)
    away = mix(place, weights, arrays, pieces, None)
    shares = mix(place, weights, arrays, pieces, send(away, OTHER))
    noise_potential = EPS * lax.dynamic_slice(all_f, (z * 4, c * 256), (4, 256)).reshape(1024)
    data_potential = EPS * lax.dynamic_index_in_dim(
        all_g.reshape(2, 4, 256), x, 1, keepdims=False
    ).reshape(512)
    shares, noise_potential, data_potential = lax.optimization_barrier(
        (shares, noise_potential, data_potential)
    )
    shares = lax.all_to_all(shares, "col", 0, 0, tiled=True)
    targets = jnp.sum(shares.reshape(4, 4, 256, 256).astype(jnp.float32), axis=1)
    targets = targets.reshape(1024, 256).astype(jnp.bfloat16)

    return (targets, noise_potential, data_potential)


def solution(mesh):
    placed = (P("row", "col"), P("col", "row"))
    return jax.shard_map(
        local,
        mesh=mesh,
        in_specs=placed,
        out_specs=(P("row", "col"), P("row"), P("col")),
        check_vma=False,
    )
```

```python
import functools

import jax
import jax.numpy as jnp
from jax import lax
from jax.experimental import pallas as pl
from jax.experimental.pallas import tpu as pltpu
from jax.sharding import PartitionSpec as P

D = 4096
ITERS = 4
COUNT = 8192
EPS = 0.02

AXES = ("row", "col")
PLACES = [(z, c, y, x) for z in range(4) for c in range(2) for y in range(4) for x in range(4)]


def flat(z, c, y, x):
    return ((z % 4 * 2 + c % 2) * 4 + y % 4) * 4 + x % 4


def pairs(move):
    return [(flat(*p), flat(*move(*p))) for p in PLACES]


def groups(shared):
    found = {}
    for p in PLACES:
        key = tuple(v for v, name in zip(p, "zcyx") if name in shared)
        found.setdefault(key, []).append(flat(*p))
    return list(found.values())


OTHER = pairs(lambda z, c, y, x: (z, c + 1, y, x))
FIRST_UP = pairs(lambda z, c, y, x: (z + 1 - c, c, y + c, x))
FIRST_DOWN = pairs(lambda z, c, y, x: (z - 1 + c, c, y - c, x))
FIRST_TWO = pairs(lambda z, c, y, x: (z + 2 - 2 * c, c, y + 2 * c, x))
SECOND_UP = pairs(lambda z, c, y, x: (z + c, c, y + 1 - c, x))
SECOND_DOWN = pairs(lambda z, c, y, x: (z - c, c, y - 1 + c, x))


def send(values, where):
    return lax.ppermute(values, AXES, where)


def spread(values, size, shared):
    copies = jnp.broadcast_to(values[None, None, :], (size, 1, values.shape[0]))
    return lax.all_to_all(
        copies, AXES, 0, 0, tiled=True, axis_index_groups=groups(shared)
    )[:, 0, :]


def lse(scores, axis):
    peak = jnp.max(scores, axis=axis, keepdims=True)
    total = jnp.sum(jnp.exp(scores - peak), axis=axis)
    return jnp.squeeze(peak, axis) + jnp.log(total)


def place_of(place, piece):
    z, c, y = place[0], place[1], place[2]
    first, second = piece
    far_z = jnp.where(c == 0, first, second)
    far_y = jnp.where(c == 0, second, first)
    return lax.rem(y + far_y, 4), lax.rem(z + far_z, 4)


BLOCKS = 8


def gram_kernel(pieces, sides, first_call, last_call, place, *refs):
    count = len(pieces)
    sources, held = refs[: len(sides)], refs[len(sides) : len(sides) + count]
    outs, state_in = refs[-3:], refs[-6:-3]
    c = place[1]
    halves = [pl.ds(pl.multiple_of(k, 256), 256) for k in (c * 256, 256 - c * 256)]
    gram, squares, noise_squares = outs
    if first_call:
        gram[...] = jnp.zeros_like(gram)
        squares[...] = jnp.zeros_like(squares)
        noise_squares[...] = jnp.zeros_like(noise_squares)
    else:
        for k in range(3):
            outs[k][...] = state_in[k][...]
    if not last_call:
        total = jnp.zeros((8, 256), jnp.float32)
        for k in range(16):
            wide = sources[0][k].astype(jnp.float32)
            total = total + jnp.sum((wide * wide).reshape(32, 8, 256), axis=0)
        noise_squares[:, halves[sides[0]]] = total
    for k, pair in enumerate(pieces):
        for side, where in enumerate(pair):
            row_group, col_group = place_of(place, where)
            rows = pl.ds(pl.multiple_of(row_group * 256, 256), 256)
            sums = [None] * len(sides)
            total = None
            for part in range(4):
                values = held[k][side * 256 : side * 256 + 256, part * 256 : part * 256 + 256]
                for n in range(len(sides)):
                    term = jnp.dot(
                        values, sources[n][part * 4 + col_group], preferred_element_type=jnp.float32
                    )
                    sums[n] = term if part == 0 else sums[n] + term
                if sides[0] == 0:
                    wide = values.astype(jnp.float32)
                    wide = wide * wide
                    folded = wide[:, :128] + wide[:, 128:]
                    total = folded if part == 0 else total + folded
            if sides[0] == 0:
                squares[rows, :] += total
            for n, half in enumerate(sides):
                gram[rows, halves[half]] += sums[n]
    if last_call:
        data_sq = jnp.sum(squares[...], axis=1, keepdims=True)
        noise_sq = jnp.sum(noise_squares[...], axis=0, keepdims=True)
        gram[...] = (2.0 * gram[...] - noise_sq - data_sq) * (1.0 / (D * EPS))


def gram_of(place, sources, sides, arrays, pieces, before, last_call):
    outs = [(1024, 512), (1024, 128), (8, 512)]
    count = len(arrays)
    operands = [*sources, *arrays, *(before or [])]
    vmem = pl.BlockSpec(memory_space=pltpu.VMEM)
    aliases = {} if before is None else {len(operands) - 2 + k: k for k in range(3)}
    return pl.pallas_call(
        functools.partial(gram_kernel, pieces, sides, before is None, last_call),
        out_shape=[jax.ShapeDtypeStruct(shape, jnp.float32) for shape in outs],
        in_specs=[pl.BlockSpec(memory_space=pltpu.SMEM)] + [vmem] * len(operands),
        out_specs=[vmem] * 3,
        input_output_aliases=aliases,
        compiler_params=pltpu.CompilerParams(vmem_limit_bytes=28 * 2**20),
        cost_estimate=pl.CostEstimate(
            flops=count * len(sides) * 2 * 512 * 256 * 1024,
            bytes_accessed=count * 2**20 + 8 * 2**20,
            transcendentals=0,
        ),
    )(place, *operands)


def mix_kernel(pieces, place, my_weights, other_weights, *refs):
    held, (out, buffer, left, sems) = refs[: 2 * BLOCKS], refs[2 * BLOCKS :]
    z, c, y = place[0], place[1], place[2]
    copies = {}
    for slot in range(2):
        for k, pair in enumerate(pieces):
            for side, where in enumerate(pair):
                far_z = jnp.where(c == slot, where[0], where[1])
                far_y = jnp.where(c == slot, where[1], where[0])
                rows = pl.ds(pl.multiple_of(slot * 1024 + lax.rem(y + far_y, 4) * 256, 256), 256)
                columns = pl.ds(pl.multiple_of(far_z * 1024, 1024), 1024)
                copies[slot, where] = pltpu.make_async_copy(
                    held[slot * BLOCKS + k].at[pl.ds(side * 256, 256)],
                    buffer.at[rows, columns],
                    sems.at[slot * 2 * BLOCKS + 2 * k + side],
                )
    order = [
        [
            [(slot, (far, k) if slot == core else (k, far)) for slot in range(2) for k in range(4)]
            for core in range(2)
        ]
        for far in range(4)
    ]
    for core in range(2):

        @pl.when(c == core)
        def _():
            for group in order:
                for name in group[core]:
                    copies[name].start()

    left[:, :1024] = my_weights[...].T
    left[:, 1024:] = other_weights[...].T
    for far, group in enumerate(order):
        for core in range(2):

            @pl.when(c == core)
            def _():
                for name in group[core]:
                    copies[name].wait()

        first = lax.rem(z + far, 4) * 4
        for part in range(4):
            values = buffer[:, (far * 4 + part) * 256 : (far * 4 + part + 1) * 256]
            total = jnp.dot(left[...], values, preferred_element_type=jnp.float32)
            out[first + part] = total.astype(out.dtype)


def mix(place, weights, arrays, pieces):
    vmem = pl.BlockSpec(memory_space=pltpu.VMEM)
    return pl.pallas_call(
        functools.partial(mix_kernel, pieces),
        out_shape=jax.ShapeDtypeStruct((16, 256, 256), jnp.bfloat16),
        in_specs=[pl.BlockSpec(memory_space=pltpu.SMEM), vmem, vmem]
        + [pl.BlockSpec(memory_space=pl.ANY)] * 2 * BLOCKS,
        out_specs=vmem,
        scratch_shapes=[
            pltpu.VMEM((2048, 4096), jnp.bfloat16),
            pltpu.VMEM((256, 2048), jnp.bfloat16),
            pltpu.SemaphoreType.DMA((4 * BLOCKS,)),
        ],
        compiler_params=pltpu.CompilerParams(vmem_limit_bytes=36 * 2**20),
        cost_estimate=pl.CostEstimate(
            flops=2 * 256 * 2048 * 4096, bytes_accessed=20 * 2**20, transcendentals=0
        ),
    )(place, *weights, *arrays)


def local(noise, data):
    row, col = lax.axis_index("row"), lax.axis_index("col")
    z, c, y, x = row // 2, row % 2, col // 4, col % 4
    place = jnp.stack([z, c, y, x]).astype(jnp.int32)

    halves = data.reshape(2, 256, 512)
    kept = lax.dynamic_index_in_dim(halves, c, 0, keepdims=False)
    came = send(lax.dynamic_index_in_dim(halves, 1 - c, 0, keepdims=False), OTHER)
    block = jnp.where(
        c == 0, jnp.concatenate([kept, came], 1), jnp.concatenate([came, kept], 1)
    )
    below, above, far = lax.optimization_barrier(
        (send(block, FIRST_UP), send(block, FIRST_DOWN), send(block, FIRST_TWO))
    )
    own = lax.all_to_all(
        jnp.swapaxes(noise.reshape(4, 256, 256), 1, 2), AXES, 0, 0, tiled=True, axis_index_groups=groups("zcx")
    )
    own = lax.all_to_all(
        jnp.broadcast_to(own[None], (4, 4, 256, 256)).reshape(4, 1024, 256),
        AXES,
        0,
        0,
        tiled=True,
        axis_index_groups=groups("zcy"),
    ).reshape(16, 256, 256)
    one, two = jnp.concatenate([block, below]), jnp.concatenate([above, far])
    one_below, two_above = send(one, SECOND_UP), send(two, SECOND_DOWN)
    one_above, two_below = send(one, SECOND_DOWN), send(two, SECOND_UP)
    one_below, two_above, one_above, two_below, own = lax.optimization_barrier(
        (one_below, two_above, one_above, two_below, own)
    )
    other = send(own, OTHER)
    one_far, two_far = send(one_below, SECOND_UP), send(two_above, SECOND_DOWN)

    arrays = [one, two, one_above, two_below, one_below, two_above, one_far, two_far]
    pieces = [
        [(first, second) for first in ((0, 3), (1, 2))[k % 2]] for k, second in enumerate((0, 0, 1, 3, 3, 1, 2, 2))
    ]
    state = gram_of(place, [own], (0,), arrays[:6], pieces[:6], None, False)
    state = gram_of(place, [other], (1,), arrays[:6], pieces[:6], state, False)
    scores = gram_of(place, [own, other], (0, 1), arrays[6:], pieces[6:], state, True)[0]

    my_scores = lax.dynamic_slice(scores, (0, c * 256), (1024, 256))
    scores_away = lax.dynamic_slice(scores, (0, 256 - c * 256), (1024, 256))
    received = []

    def row_exchange(g, extra):
        mine = lse(scores + g[:, None], 0)
        shared = spread(jnp.concatenate([mine, extra]), 8, "zy")
        return lse(shared[:, :512], 0), shared[:, 512:]

    def col_exchange(f, extra):
        mine = lse(scores + f[None, :], 1)
        shared = spread(jnp.concatenate([mine, extra]), 16, "cx")
        return lse(shared[:, :1024], 0), shared[:, 1024:]

    log_count = jnp.log(float(COUNT))
    nothing = jnp.zeros((0,), jnp.float32)
    g = jnp.zeros((1024,), jnp.float32)
    for step in range(ITERS):
        f = -log_count - row_exchange(g, nothing)[0]
        total, all_f = col_exchange(f, nothing if step < ITERS - 1 else f)
        g = -log_count - total
        if step < ITERS - 1:
            queue = [scores_away, *arrays[2:], *arrays[:2]][3 * step : 3 * step + 3]
            g, *queue = lax.optimization_barrier((g, *[send(values, OTHER) for values in queue]))
            received += queue
    norm, all_g = row_exchange(g, g)
    all_g = lax.dynamic_index_in_dim(all_g.reshape(2, 4, 1024), x, 1, keepdims=False)
    g_other = lax.dynamic_index_in_dim(all_g, 1 - c, 0, keepdims=False)
    norm = lax.dynamic_slice(norm, (c * 256,), (256,))
    other_scores, *other_arrays = received
    other_arrays = other_arrays[6:] + other_arrays[:6]
    weights = [
        jnp.exp(part + potential[:, None] - norm[None, :]).astype(jnp.bfloat16)
        for part, potential in ((my_scores, g), (other_scores, g_other))
    ]
    shares = mix(place, weights, arrays + other_arrays, pieces)
    noise_potential = EPS * lax.dynamic_slice(all_f, (z * 4, c * 256), (4, 256)).reshape(1024)
    data_potential = EPS * lax.dynamic_slice(all_g, (0, y * 256), (2, 256)).reshape(512)
    shares, noise_potential, data_potential = lax.optimization_barrier(
        (shares, noise_potential, data_potential)
    )
    shares = lax.all_to_all(shares, "col", 0, 0, tiled=True)
    targets = jnp.sum(shares.reshape(4, 4, 256, 256).astype(jnp.float32), axis=1)
    targets = targets.reshape(1024, 256).astype(jnp.bfloat16)

    return (targets, noise_potential, data_potential)


def solution(mesh):
    placed = (P("row", "col"), P("col", "row"))
    return jax.shard_map(
        local,
        mesh=mesh,
        in_specs=placed,
        out_specs=(P("row", "col"), P("row"), P("col")),
        check_vma=False,
    )
```

```python
import functools

import jax
import jax.numpy as jnp
from jax import lax
from jax.experimental import pallas as pl
from jax.experimental.pallas import tpu as pltpu
from jax.sharding import PartitionSpec as P

D = 4096
ITERS = 4
COUNT = 8192
EPS = 0.02

AXES = ("row", "col")
PLACES = [(z, c, y, x) for z in range(4) for c in range(2) for y in range(4) for x in range(4)]


def flat(z, c, y, x):
    return ((z % 4 * 2 + c % 2) * 4 + y % 4) * 4 + x % 4


def pairs(move):
    return [(flat(*p), flat(*move(*p))) for p in PLACES]


def groups(shared):
    found = {}
    for p in PLACES:
        key = tuple(v for v, name in zip(p, "zcyx") if name in shared)
        found.setdefault(key, []).append(flat(*p))
    return list(found.values())


OTHER = pairs(lambda z, c, y, x: (z, c + 1, y, x))
FIRST_UP = pairs(lambda z, c, y, x: (z + 1 - c, c, y + c, x))
FIRST_DOWN = pairs(lambda z, c, y, x: (z - 1 + c, c, y - c, x))
FIRST_TWO = pairs(lambda z, c, y, x: (z + 2 - 2 * c, c, y + 2 * c, x))
SECOND_UP = pairs(lambda z, c, y, x: (z + c, c, y + 1 - c, x))
SECOND_DOWN = pairs(lambda z, c, y, x: (z - c, c, y - 1 + c, x))


def send(values, where):
    return lax.ppermute(values, AXES, where)


def spread(values, size, shared):
    copies = jnp.broadcast_to(values[None, None, :], (size, 1, values.shape[0]))
    return lax.all_to_all(
        copies, AXES, 0, 0, tiled=True, axis_index_groups=groups(shared)
    )[:, 0, :]


def lse(scores, axis):
    peak = jnp.max(scores, axis=axis, keepdims=True)
    total = jnp.sum(jnp.exp(scores - peak), axis=axis)
    return jnp.squeeze(peak, axis) + jnp.log(total)


def place_of(place, piece):
    z, c, y = place[0], place[1], place[2]
    first, second = piece
    far_z = jnp.where(c == 0, first, second)
    far_y = jnp.where(c == 0, second, first)
    return lax.rem(y + far_y, 4), lax.rem(z + far_z, 4)


BLOCKS = 8


def gram_kernel(pieces, sides, first_call, last_call, place, *refs):
    count = len(pieces)
    sources, held = refs[: len(sides)], refs[len(sides) : len(sides) + count]
    outs, state_in = refs[-3:], refs[-6:-3]
    c = place[1]
    halves = [pl.ds(pl.multiple_of(k, 256), 256) for k in (c * 256, 256 - c * 256)]
    gram, squares, noise_squares = outs
    if first_call:
        gram[...] = jnp.zeros_like(gram)
        squares[...] = jnp.zeros_like(squares)
        noise_squares[...] = jnp.zeros_like(noise_squares)
    else:
        for k in range(3):
            outs[k][...] = state_in[k][...]
    if not last_call:
        total = jnp.zeros((8, 256), jnp.float32)
        for k in range(16):
            wide = sources[0][k].astype(jnp.float32)
            total = total + jnp.sum((wide * wide).reshape(32, 8, 256), axis=0)
        noise_squares[:, halves[sides[0]]] = total
    for k, pair in enumerate(pieces):
        for side, where in enumerate(pair):
            row_group, col_group = place_of(place, where)
            rows = pl.ds(pl.multiple_of(row_group * 256, 256), 256)
            sums = [None] * len(sides)
            total = None
            for part in range(4):
                values = held[k][side * 256 : side * 256 + 256, part * 256 : part * 256 + 256]
                for n in range(len(sides)):
                    term = jnp.dot(
                        values, sources[n][part * 4 + col_group], preferred_element_type=jnp.float32
                    )
                    sums[n] = term if part == 0 else sums[n] + term
                if sides[0] == 0:
                    wide = values.astype(jnp.float32)
                    wide = wide * wide
                    folded = wide[:, :128] + wide[:, 128:]
                    total = folded if part == 0 else total + folded
            if sides[0] == 0:
                squares[rows, :] += total
            for n, half in enumerate(sides):
                gram[rows, halves[half]] += sums[n]
    if last_call:
        data_sq = jnp.sum(squares[...], axis=1, keepdims=True)
        noise_sq = jnp.sum(noise_squares[...], axis=0, keepdims=True)
        gram[...] = (2.0 * gram[...] - noise_sq - data_sq) * (1.0 / (D * EPS))


def gram_of(place, sources, sides, arrays, pieces, before, last_call):
    outs = [(1024, 512), (1024, 128), (8, 512)]
    count = len(arrays)
    operands = [*sources, *arrays, *(before or [])]
    vmem = pl.BlockSpec(memory_space=pltpu.VMEM)
    aliases = {} if before is None else {len(operands) - 2 + k: k for k in range(3)}
    return pl.pallas_call(
        functools.partial(gram_kernel, pieces, sides, before is None, last_call),
        out_shape=[jax.ShapeDtypeStruct(shape, jnp.float32) for shape in outs],
        in_specs=[pl.BlockSpec(memory_space=pltpu.SMEM)] + [vmem] * len(operands),
        out_specs=[vmem] * 3,
        input_output_aliases=aliases,
        compiler_params=pltpu.CompilerParams(vmem_limit_bytes=28 * 2**20),
        cost_estimate=pl.CostEstimate(
            flops=count * len(sides) * 2 * 512 * 256 * 1024,
            bytes_accessed=count * 2**20 + 8 * 2**20,
            transcendentals=0,
        ),
    )(place, *operands)


def mix_kernel(pieces, place, my_weights, other_weights, *refs):
    held, (out, buffer, left, sems) = refs[: 2 * BLOCKS], refs[2 * BLOCKS :]
    z, c, y = place[0], place[1], place[2]
    copies = {}
    for slot in range(2):
        for k, pair in enumerate(pieces):
            for side, where in enumerate(pair):
                far_z = jnp.where(c == slot, where[0], where[1])
                far_y = jnp.where(c == slot, where[1], where[0])
                rows = pl.ds(pl.multiple_of(slot * 1024 + lax.rem(y + far_y, 4) * 256, 256), 256)
                columns = pl.ds(pl.multiple_of(far_z * 1024, 1024), 1024)
                copies[slot, where] = pltpu.make_async_copy(
                    held[slot * BLOCKS + k].at[pl.ds(side * 256, 256)],
                    buffer.at[rows, columns],
                    sems.at[slot * 2 * BLOCKS + 2 * k + side],
                )
    order = [
        [
            [(slot, (far, k) if slot == core else (k, far)) for slot in range(2) for k in range(4)]
            for core in range(2)
        ]
        for far in range(4)
    ]
    for core in range(2):

        @pl.when(c == core)
        def _():
            for group in order:
                for name in group[core]:
                    copies[name].start()

    left[:, :1024] = my_weights[...].T
    left[:, 1024:] = other_weights[...].T
    for far, group in enumerate(order):
        for core in range(2):

            @pl.when(c == core)
            def _():
                for name in group[core]:
                    copies[name].wait()

        first = lax.rem(z + far, 4) * 4
        for part in range(4):
            values = buffer[:, (far * 4 + part) * 256 : (far * 4 + part + 1) * 256]
            total = jnp.dot(left[...], values, preferred_element_type=jnp.float32)
            out[first + part] = total.astype(out.dtype)


def mix(place, weights, arrays, pieces):
    vmem = pl.BlockSpec(memory_space=pltpu.VMEM)
    return pl.pallas_call(
        functools.partial(mix_kernel, pieces),
        out_shape=jax.ShapeDtypeStruct((16, 256, 256), jnp.bfloat16),
        in_specs=[pl.BlockSpec(memory_space=pltpu.SMEM), vmem, vmem]
        + [pl.BlockSpec(memory_space=pl.ANY)] * 2 * BLOCKS,
        out_specs=vmem,
        scratch_shapes=[
            pltpu.VMEM((2048, 4096), jnp.bfloat16),
            pltpu.VMEM((256, 2048), jnp.bfloat16),
            pltpu.SemaphoreType.DMA((4 * BLOCKS,)),
        ],
        compiler_params=pltpu.CompilerParams(vmem_limit_bytes=36 * 2**20),
        cost_estimate=pl.CostEstimate(
            flops=2 * 256 * 2048 * 4096, bytes_accessed=20 * 2**20, transcendentals=0
        ),
    )(place, *weights, *arrays)


def local(noise, data):
    row, col = lax.axis_index("row"), lax.axis_index("col")
    z, c, y, x = row // 2, row % 2, col // 4, col % 4
    place = jnp.stack([z, c, y, x]).astype(jnp.int32)

    halves = data.reshape(2, 256, 512)
    kept = lax.dynamic_index_in_dim(halves, c, 0, keepdims=False)
    came = send(halves, OTHER)
    came = lax.dynamic_index_in_dim(came, c, 0, keepdims=False)
    block = jnp.where(
        c == 0, jnp.concatenate([kept, came], 1), jnp.concatenate([came, kept], 1)
    )
    below, above, far = lax.optimization_barrier(
        (send(block, FIRST_UP), send(block, FIRST_DOWN), send(block, FIRST_TWO))
    )
    own = lax.all_to_all(
        jnp.swapaxes(noise.reshape(4, 256, 256), 1, 2), AXES, 0, 0, tiled=True, axis_index_groups=groups("zcx")
    )
    own = lax.all_to_all(
        jnp.broadcast_to(own[None], (4, 4, 256, 256)).reshape(4, 1024, 256),
        AXES,
        0,
        0,
        tiled=True,
        axis_index_groups=groups("zcy"),
    ).reshape(16, 256, 256)
    one, two = jnp.concatenate([block, below]), jnp.concatenate([above, far])
    one_below, two_above = send(one, SECOND_UP), send(two, SECOND_DOWN)
    one_above, two_below = send(one, SECOND_DOWN), send(two, SECOND_UP)
    one_below, two_above, one_above, two_below, own = lax.optimization_barrier(
        (one_below, two_above, one_above, two_below, own)
    )
    other = send(own, OTHER)
    one_far, two_far = send(one_below, SECOND_UP), send(two_above, SECOND_DOWN)

    arrays = [one, two, one_above, two_below, one_below, two_above, one_far, two_far]
    pieces = [
        [(first, second) for first in ((0, 3), (1, 2))[k % 2]] for k, second in enumerate((0, 0, 1, 3, 3, 1, 2, 2))
    ]
    state = gram_of(place, [own], (0,), arrays[:6], pieces[:6], None, False)
    state = gram_of(place, [other], (1,), arrays[:6], pieces[:6], state, False)
    scores = gram_of(place, [own, other], (0, 1), arrays[6:], pieces[6:], state, True)[0]

    my_scores = lax.dynamic_slice(scores, (0, c * 256), (1024, 256))
    scores_away = lax.dynamic_slice(scores, (0, 256 - c * 256), (1024, 256))
    received = []

    def row_exchange(g, extra):
        mine = lse(scores + g[:, None], 0)
        shared = spread(jnp.concatenate([mine, extra]), 8, "zy")
        return lse(shared[:, :512], 0), shared[:, 512:]

    def col_exchange(f, extra):
        mine = lse(scores + f[None, :], 1)
        shared = spread(jnp.concatenate([mine, extra]), 16, "cx")
        return lse(shared[:, :1024], 0), shared[:, 1024:]

    log_count = jnp.log(float(COUNT))
    nothing = jnp.zeros((0,), jnp.float32)
    g = jnp.zeros((1024,), jnp.float32)
    for step in range(ITERS):
        f = -log_count - row_exchange(g, nothing)[0]
        total, all_f = col_exchange(f, nothing if step < ITERS - 1 else f)
        g = -log_count - total
        if step < ITERS - 1:
            queue = [scores_away, *arrays[2:], *arrays[:2]][(0, 5, 9)[step] : (5, 9, 9)[step]]
            g, *queue = lax.optimization_barrier((g, *[send(values, OTHER) for values in queue]))
            received += queue
    norm, all_g = row_exchange(g, g)
    all_g = lax.dynamic_index_in_dim(all_g.reshape(2, 4, 1024), x, 1, keepdims=False)
    g_other = lax.dynamic_index_in_dim(all_g, 1 - c, 0, keepdims=False)
    norm = lax.dynamic_slice(norm, (c * 256,), (256,))
    other_scores, *other_arrays = received
    other_arrays = other_arrays[6:] + other_arrays[:6]
    weights = [
        jnp.exp(part + potential[:, None] - norm[None, :]).astype(jnp.bfloat16)
        for part, potential in ((my_scores, g), (other_scores, g_other))
    ]
    shares = mix(place, weights, arrays + other_arrays, pieces)
    noise_potential = EPS * lax.dynamic_slice(all_f, (z * 4, c * 256), (4, 256)).reshape(1024)
    data_potential = EPS * lax.dynamic_slice(all_g, (0, y * 256), (2, 256)).reshape(512)
    shares, noise_potential, data_potential = lax.optimization_barrier(
        (shares, noise_potential, data_potential)
    )
    shares = lax.all_to_all(shares, "col", 0, 0, tiled=True)
    targets = jnp.sum(shares.reshape(4, 4, 256, 256).astype(jnp.float32), axis=1)
    targets = targets.reshape(1024, 256).astype(jnp.bfloat16)

    return (targets, noise_potential, data_potential)


def solution(mesh):
    placed = (P("row", "col"), P("col", "row"))
    return jax.shard_map(
        local,
        mesh=mesh,
        in_specs=placed,
        out_specs=(P("row", "col"), P("row"), P("col")),
        check_vma=False,
    )
```

```python
import functools

import jax
import jax.numpy as jnp
from jax import lax
from jax.experimental import pallas as pl
from jax.experimental.pallas import tpu as pltpu
from jax.sharding import PartitionSpec as P

D = 4096
ITERS = 4
COUNT = 8192
EPS = 0.02

AXES = ("row", "col")
PLACES = [(z, c, y, x) for z in range(4) for c in range(2) for y in range(4) for x in range(4)]


def flat(z, c, y, x):
    return ((z % 4 * 2 + c % 2) * 4 + y % 4) * 4 + x % 4


def pairs(move):
    return [(flat(*p), flat(*move(*p))) for p in PLACES]


def groups(shared):
    found = {}
    for p in PLACES:
        key = tuple(v for v, name in zip(p, "zcyx") if name in shared)
        found.setdefault(key, []).append(flat(*p))
    return list(found.values())


OTHER = pairs(lambda z, c, y, x: (z, c + 1, y, x))
FIRST_UP = pairs(lambda z, c, y, x: (z + 1 - c, c, y + c, x))
FIRST_DOWN = pairs(lambda z, c, y, x: (z - 1 + c, c, y - c, x))
FIRST_TWO = pairs(lambda z, c, y, x: (z + 2 - 2 * c, c, y + 2 * c, x))
SECOND_UP = pairs(lambda z, c, y, x: (z + c, c, y + 1 - c, x))
SECOND_DOWN = pairs(lambda z, c, y, x: (z - c, c, y - 1 + c, x))


def send(values, where):
    return lax.ppermute(values, AXES, where)


def spread(values, size, shared):
    copies = jnp.broadcast_to(values[None, None, :], (size, 1, values.shape[0]))
    return lax.all_to_all(
        copies, AXES, 0, 0, tiled=True, axis_index_groups=groups(shared)
    )[:, 0, :]


def lse(scores, axis):
    peak = jnp.max(scores, axis=axis, keepdims=True)
    total = jnp.sum(jnp.exp(scores - peak), axis=axis)
    return jnp.squeeze(peak, axis) + jnp.log(total)


def place_of(place, piece):
    z, c, y = place[0], place[1], place[2]
    first, second = piece
    far_z = jnp.where(c == 0, first, second)
    far_y = jnp.where(c == 0, second, first)
    return lax.rem(y + far_y, 4), lax.rem(z + far_z, 4)


BLOCKS = 8


def gram_kernel(pieces, sides, first_call, last_call, place, *refs):
    count = len(pieces)
    sources, held = refs[: len(sides)], refs[len(sides) : len(sides) + count]
    outs, state_in = refs[-3:], refs[-6:-3]
    c = place[1]
    halves = [pl.ds(pl.multiple_of(k, 256), 256) for k in (c * 256, 256 - c * 256)]
    gram, squares, noise_squares = outs
    if first_call:
        gram[...] = jnp.zeros_like(gram)
        squares[...] = jnp.zeros_like(squares)
        noise_squares[...] = jnp.zeros_like(noise_squares)
    else:
        for k in range(3):
            outs[k][...] = state_in[k][...]
    if not last_call:
        total = jnp.zeros((8, 256), jnp.float32)
        for k in range(16):
            wide = sources[0][k].astype(jnp.float32)
            total = total + jnp.sum((wide * wide).reshape(32, 8, 256), axis=0)
        noise_squares[:, halves[sides[0]]] = total
    for k, pair in enumerate(pieces):
        for side, where in enumerate(pair):
            row_group, col_group = place_of(place, where)
            rows = pl.ds(pl.multiple_of(row_group * 256, 256), 256)
            sums = [None] * len(sides)
            total = None
            for part in range(4):
                values = held[k][side * 256 : side * 256 + 256, part * 256 : part * 256 + 256]
                for n in range(len(sides)):
                    term = jnp.dot(
                        values, sources[n][part * 4 + col_group], preferred_element_type=jnp.float32
                    )
                    sums[n] = term if part == 0 else sums[n] + term
                if sides[0] == 0:
                    wide = values.astype(jnp.float32)
                    wide = wide * wide
                    folded = wide[:, :128] + wide[:, 128:]
                    total = folded if part == 0 else total + folded
            if sides[0] == 0:
                squares[rows, :] += total
            for n, half in enumerate(sides):
                gram[rows, halves[half]] += sums[n]
    if last_call:
        data_sq = jnp.sum(squares[...], axis=1, keepdims=True)
        noise_sq = jnp.sum(noise_squares[...], axis=0, keepdims=True)
        gram[...] = (2.0 * gram[...] - noise_sq - data_sq) * (1.0 / (D * EPS))


def gram_of(place, sources, sides, arrays, pieces, before, last_call):
    outs = [(1024, 512), (1024, 128), (8, 512)]
    count = len(arrays)
    operands = [*sources, *arrays, *(before or [])]
    vmem = pl.BlockSpec(memory_space=pltpu.VMEM)
    aliases = {} if before is None else {len(operands) - 2 + k: k for k in range(3)}
    return pl.pallas_call(
        functools.partial(gram_kernel, pieces, sides, before is None, last_call),
        out_shape=[jax.ShapeDtypeStruct(shape, jnp.float32) for shape in outs],
        in_specs=[pl.BlockSpec(memory_space=pltpu.SMEM)] + [vmem] * len(operands),
        out_specs=[vmem] * 3,
        input_output_aliases=aliases,
        compiler_params=pltpu.CompilerParams(vmem_limit_bytes=28 * 2**20),
        cost_estimate=pl.CostEstimate(
            flops=count * len(sides) * 2 * 512 * 256 * 1024,
            bytes_accessed=count * 2**20 + 8 * 2**20,
            transcendentals=0,
        ),
    )(place, *operands)


def mix_kernel(pieces, place, my_weights, other_weights, *refs):
    held, (out, buffer, left, sems) = refs[: 2 * BLOCKS], refs[2 * BLOCKS :]
    z, c, y = place[0], place[1], place[2]
    copies = {}
    for slot in range(2):
        for k, pair in enumerate(pieces):
            for side, where in enumerate(pair):
                far_z = jnp.where(c == slot, where[0], where[1])
                far_y = jnp.where(c == slot, where[1], where[0])
                rows = pl.ds(pl.multiple_of(slot * 1024 + lax.rem(y + far_y, 4) * 256, 256), 256)
                columns = pl.ds(pl.multiple_of(far_z * 1024, 1024), 1024)
                copies[slot, where] = pltpu.make_async_copy(
                    held[slot * BLOCKS + k].at[pl.ds(side * 256, 256)],
                    buffer.at[rows, columns],
                    sems.at[slot * 2 * BLOCKS + 2 * k + side],
                )
    order = [
        [
            [(slot, (far, k) if slot == core else (k, far)) for slot in range(2) for k in range(4)]
            for core in range(2)
        ]
        for far in range(4)
    ]
    for core in range(2):

        @pl.when(c == core)
        def _():
            for group in order:
                for name in group[core]:
                    copies[name].start()

    left[:, :1024] = my_weights[...].T
    left[:, 1024:] = other_weights[...].T
    for far, group in enumerate(order):
        for core in range(2):

            @pl.when(c == core)
            def _():
                for name in group[core]:
                    copies[name].wait()

        first = lax.rem(z + far, 4) * 4
        for part in range(4):
            values = buffer[:, (far * 4 + part) * 256 : (far * 4 + part + 1) * 256]
            total = jnp.dot(left[...], values, preferred_element_type=jnp.float32)
            out[first + part] = total.astype(out.dtype)


def mix(place, weights, arrays, pieces):
    vmem = pl.BlockSpec(memory_space=pltpu.VMEM)
    return pl.pallas_call(
        functools.partial(mix_kernel, pieces),
        out_shape=jax.ShapeDtypeStruct((16, 256, 256), jnp.bfloat16),
        in_specs=[pl.BlockSpec(memory_space=pltpu.SMEM), vmem, vmem]
        + [pl.BlockSpec(memory_space=pl.ANY)] * 2 * BLOCKS,
        out_specs=vmem,
        scratch_shapes=[
            pltpu.VMEM((2048, 4096), jnp.bfloat16),
            pltpu.VMEM((256, 2048), jnp.bfloat16),
            pltpu.SemaphoreType.DMA((4 * BLOCKS,)),
        ],
        compiler_params=pltpu.CompilerParams(vmem_limit_bytes=36 * 2**20),
        cost_estimate=pl.CostEstimate(
            flops=2 * 256 * 2048 * 4096, bytes_accessed=20 * 2**20, transcendentals=0
        ),
    )(place, *weights, *arrays)


def local(noise, data):
    row, col = lax.axis_index("row"), lax.axis_index("col")
    z, c, y, x = row // 2, row % 2, col // 4, col % 4
    place = jnp.stack([z, c, y, x]).astype(jnp.int32)

    halves = data.reshape(2, 256, 512)
    kept = lax.dynamic_index_in_dim(halves, c, 0, keepdims=False)
    came = send(halves, OTHER)
    came = lax.dynamic_index_in_dim(came, c, 0, keepdims=False)
    block = jnp.where(
        c == 0, jnp.concatenate([kept, came], 1), jnp.concatenate([came, kept], 1)
    )
    below, above, far = lax.optimization_barrier(
        (send(block, FIRST_UP), send(block, FIRST_DOWN), send(block, FIRST_TWO))
    )
    own = lax.all_to_all(
        jnp.swapaxes(noise.reshape(4, 256, 256), 1, 2), AXES, 0, 0, tiled=True, axis_index_groups=groups("zcx")
    )
    own = lax.all_to_all(
        jnp.broadcast_to(own[None], (4, 4, 256, 256)).reshape(4, 1024, 256),
        AXES,
        0,
        0,
        tiled=True,
        axis_index_groups=groups("zcy"),
    ).reshape(16, 256, 256)
    one, two = jnp.concatenate([block, below]), jnp.concatenate([above, far])
    one_below, two_above = send(one, SECOND_UP), send(two, SECOND_DOWN)
    one_above, two_below = send(one, SECOND_DOWN), send(two, SECOND_UP)
    one_below, two_above, one_above, two_below, own = lax.optimization_barrier(
        (one_below, two_above, one_above, two_below, own)
    )
    other = send(own, OTHER)
    one_far, two_far = send(one_below, SECOND_UP), send(two_above, SECOND_DOWN)

    arrays = [one, two, one_above, two_below, one_below, two_above, one_far, two_far]
    pieces = [
        [(first, second) for first in ((0, 3), (1, 2))[k % 2]] for k, second in enumerate((0, 0, 1, 3, 3, 1, 2, 2))
    ]
    state = gram_of(place, [own], (0,), arrays[:6], pieces[:6], None, False)
    state = gram_of(place, [other], (1,), arrays[:6], pieces[:6], state, False)
    scores = gram_of(place, [own, other], (0, 1), arrays[6:], pieces[6:], state, True)[0]

    my_scores = lax.dynamic_slice(scores, (0, c * 256), (1024, 256))
    scores_away = lax.dynamic_slice(scores, (0, 256 - c * 256), (1024, 256))
    received = []

    def row_exchange(g, extra):
        mine = lse(scores + g[:, None], 0)
        shared = spread(jnp.concatenate([mine, extra]), 8, "zy")
        return lse(shared[:, :512], 0), shared[:, 512:]

    def col_exchange(f, extra):
        mine = lse(scores + f[None, :], 1)
        shared = spread(jnp.concatenate([mine, extra]), 16, "cx")
        return lse(shared[:, :1024], 0), shared[:, 1024:]

    log_count = jnp.log(float(COUNT))
    nothing = jnp.zeros((0,), jnp.float32)
    g = jnp.zeros((1024,), jnp.float32)
    for step in range(ITERS):
        f = -log_count - row_exchange(g, nothing)[0]
        total, all_f = col_exchange(f, nothing if step < ITERS - 1 else f)
        g = -log_count - total
        if step < ITERS - 1:
            queue = [scores_away, *arrays[2:], *arrays[:2]][(0, 5, 9)[step] : (5, 9, 9)[step]]
            g, *queue = lax.optimization_barrier((g, *[send(values, OTHER) for values in queue]))
            received += queue
        if step == 0:
            g, my_scores = lax.optimization_barrier((g, my_scores))
    norm, all_g = row_exchange(g, g)
    all_g = lax.dynamic_index_in_dim(all_g.reshape(2, 4, 1024), x, 1, keepdims=False)
    g_other = lax.dynamic_index_in_dim(all_g, 1 - c, 0, keepdims=False)
    norm = lax.dynamic_slice(norm, (c * 256,), (256,))
    other_scores, *other_arrays = received
    other_arrays = other_arrays[6:] + other_arrays[:6]
    weights = [
        jnp.exp(part + potential[:, None] - norm[None, :]).astype(jnp.bfloat16)
        for part, potential in ((my_scores, g), (other_scores, g_other))
    ]
    shares = mix(place, weights, arrays + other_arrays, pieces)
    noise_potential = EPS * lax.dynamic_slice(all_f, (z * 4, c * 256), (4, 256)).reshape(1024)
    data_potential = EPS * lax.dynamic_slice(all_g, (0, y * 256), (2, 256)).reshape(512)
    shares, noise_potential, data_potential = lax.optimization_barrier(
        (shares, noise_potential, data_potential)
    )
    shares = lax.all_to_all(shares, "col", 0, 0, tiled=True)
    targets = jnp.sum(shares.reshape(4, 4, 256, 256).astype(jnp.float32), axis=1)
    targets = targets.reshape(1024, 256).astype(jnp.bfloat16)

    return (targets, noise_potential, data_potential)


def solution(mesh):
    placed = (P("row", "col"), P("col", "row"))
    return jax.shard_map(
        local,
        mesh=mesh,
        in_specs=placed,
        out_specs=(P("row", "col"), P("row"), P("col")),
        check_vma=False,
    )
```
